256 devices in a mesh: rows: 8 (over z_lo, core), cols: 32 (over y, x, z_hi).
Axes of the slice: x: 4, y: 4, z: 8 (z_hi: 2, z_lo: 4; z = z_hi * 4 + z_lo), core: 2. Of those that a mesh axis runs over, the one named last changes fastest.
Arguments:
- orbitals: bfloat16 [32768, 16384], P('rows', 'cols'), may hold values from -0.4453125 to 0.4453125
- applied: bfloat16 [32768, 16384], P('rows', 'cols'), may hold values from -0.4453125 to 0.4453125
Outputs:
- gram_blocks: float32 [3, 16384, 512], P(None, 'cols')
- ham_blocks: float32 [3, 16384, 512], P(None, 'cols')
The draws below stay inside these ranges and needn't reach their ends.
All inputs are finite; a program needn't handle non-finite values.
Results may differ from the reference program's by a relative error of at most 0.0003.
Values may be sent and summed in bfloat16 or wider, within the bound.
A program may use at most 128 MiB of HBM per device.

```python
import jax
import jax.numpy as jnp
from jax import lax

BLOCK = 512
ROUNDS = 2
GRID = 32768
ORBITALS = 16384
N_COLS = 32


def level_of(own_key, dims, pieces, least, high):
    gain, own = 1.0, jax.random.fold_in(own_key, 6)
    for dim, shards_of in pieces:
        heights = jnp.exp(jax.random.uniform(jax.random.fold_in(own, dim), (shards_of,), jnp.float32, least / len(pieces), high / len(pieces)))
        gain = gain * jnp.repeat(heights, dims[dim] // shards_of).reshape([-1 if axis == dim else 1 for axis in range(len(dims))])
    return gain


def normal_values(rng, dims, width, reach, split=(), kind=jnp.bfloat16):
    drawn = jax.random.normal(rng, dims, jnp.float32) * width
    if len(split) > 0:
        drawn = level_of(rng, dims, split, -0.22, 0.18) * drawn
    return jnp.clip(drawn, min=-reach, max=reach).astype(kind)


def setup_inputs(seed: int = 0) -> dict:
    key_of = jax.random.split(jax.random.key(seed), 3)
    return {
        "orbitals": normal_values(key_of[0], (GRID, ORBITALS), (GRID ** -0.25), 0.4453125, ((0, 8), (1, 32))),
        "applied": normal_values(key_of[1], (GRID, ORBITALS), (GRID ** -0.25), 0.4453125, ((0, 8), (1, 32))),
    }


def reference(orbitals, applied):
    def one_block(c):
        own = lax.dynamic_slice_in_dim(orbitals, c * BLOCK, BLOCK, 1)
        own_applied = lax.dynamic_slice_in_dim(applied, c * BLOCK, BLOCK, 1)
        gram_list = []
        ham_list = []
        for step in range(ROUNDS + 1):
            start = (((c - step) % N_COLS) * BLOCK).astype(jnp.int32)
            other = lax.dynamic_slice_in_dim(orbitals, start, BLOCK, 1)
            gram_list.append(jnp.dot(own.T, other, preferred_element_type=jnp.float32))
            ham_list.append(jnp.dot(other.T, own_applied, preferred_element_type=jnp.float32))
        return jnp.stack(gram_list), jnp.stack(ham_list)

    gram, ham = lax.map(one_block, jnp.arange(N_COLS, dtype=jnp.int32))
    gram = gram.transpose(1, 0, 2, 3).reshape(ROUNDS + 1, N_COLS * BLOCK, BLOCK)
    ham = ham.transpose(1, 0, 2, 3).reshape(ROUNDS + 1, N_COLS * BLOCK, BLOCK)
    return gram, ham
```

```python
import functools

import jax
import jax.numpy as jnp
from jax import lax
from jax.experimental import pallas as pl
from jax.experimental.pallas import tpu as pltpu
from jax.sharding import PartitionSpec as P

BLOCK = 512
GRID_ROWS = 4096
STRIP = 128
CHUNKS = BLOCK // STRIP
PIECE = 512
PER_CHUNK = GRID_ROWS // PIECE
PIECES = CHUNKS * PER_CHUNK
ROUND_OF = (0, 2, 1)
UNITS = 3 * CHUNKS
AHEAD = 3
LAG = AHEAD + 2
KTILE = 512
ROWS_AT_ONCE = 16
MESH = pl.DeviceIdType.MESH


def plan():
    ready = {}
    for j in range(CHUNKS):
        ready[j] = j
        ready[CHUNKS + j] = 4 * j + 7
        ready[2 * CHUNKS + j] = PER_CHUNK * (j + 1) + AHEAD + 1
    stages = []
    for unit, at in ready.items():
        for stage, delay in enumerate((0, 1, 1 + LAG, 1 + 2 * LAG, 1 + 3 * LAG)):
            stages.append((at + delay, stage, unit))
    return sorted(stages)


def kernel(n_cols, x_ref, hx_ref, out_ref, blocks, both, part, sib_in, snd, rcv, fin,
           load_sem, r1_send, r1_recv, r2_send, r2_recv, sib_send, sib_recv,
           z_send, z_recv, fin_send, fin_recv, out_sem):
    row = lax.axis_index("rows")
    col = lax.axis_index("cols")
    core = lax.rem(row, 2)
    z = row // 2
    upper = lax.rem(col, 2)
    edge = jnp.logical_or(z == 0, z == 3)
    inner = jnp.logical_or(z == 1, z == 2)
    sibling = (row + 1 - 2 * core, col)
    beside = (row + 2 - 4 * lax.rem(z, 2), col)
    across = ((3 - z) * 2 + core, col)
    half = (row, col + 1 - 2 * upper)
    ahead = (row, lax.rem(col + 2, n_cols))
    behind = (row, lax.rem(col + n_cols - 2, n_cols))

    loads = []
    for j in range(CHUNKS):
        loads.append(pltpu.make_async_copy(
            x_ref.at[:, pl.ds(j * STRIP, STRIP)], blocks.at[j], load_sem.at[j]))
    loads.append(pltpu.make_async_copy(x_ref, both.at[:, pl.ds(0, BLOCK)], load_sem.at[CHUNKS]))
    loads.append(pltpu.make_async_copy(hx_ref, both.at[:, pl.ds(BLOCK, BLOCK)], load_sem.at[CHUNKS + 1]))
    for load in loads:
        load.start()

    barrier = pltpu.get_barrier_semaphore()
    for device in (sibling, beside, across, half, ahead, behind):
        pl.semaphore_signal(barrier, inc=1, device_id=device, device_id_type=MESH)
    pl.semaphore_wait(barrier, 6)

    def piece(slot, p):
        return blocks.at[slot + p // PER_CHUNK, pl.ds((p % PER_CHUNK) * PIECE, PIECE)]

    def remote(src, dst, send, recv, device):
        return pltpu.make_async_remote_copy(
            src_ref=src, dst_ref=dst, send_sem=send, recv_sem=recv,
            device_id=device, device_id_type=MESH)

    def two_back(p):
        return remote(piece(0, p), piece(CHUNKS, p), r2_send.at[p], r2_recv.at[p], ahead)

    def one_back(p):
        return remote(piece(upper * CHUNKS, p), piece(2 * CHUNKS, p), r1_send.at[p], r1_recv.at[p], half)

    def to_sibling(u):
        return remote(part.at[u, 1 - core], sib_in.at[u], sib_send.at[u], sib_recv.at[u], sibling)

    def edge_to_inner(u):
        return remote(snd.at[0, u], rcv.at[0, u], z_send.at[0, u], z_recv.at[0, u], beside)

    def inner_to_inner(u):
        return remote(snd.at[0, u], rcv.at[1, u], z_send.at[0, u], z_recv.at[1, u], across)

    def inner_to_edge(u):
        return remote(snd.at[1, u], rcv.at[0, u], z_send.at[1, u], z_recv.at[0, u], beside)

    def place(u):
        return out_ref.at[core, ROUND_OF[u // CHUNKS], pl.ds((u % CHUNKS) * STRIP, STRIP)]

    def fin_to_sibling(u):
        return remote(fin.at[u], place(u), fin_send.at[u], fin_recv.at[u], sibling)

    def fin_to_out(u):
        return pltpu.make_async_copy(fin.at[u], place(u), out_sem.at[u])

    def by_rows(body):
        @pl.loop(0, STRIP // ROWS_AT_ONCE)
        def _(i):
            body(pl.ds(pl.multiple_of(i * ROWS_AT_ONCE, ROWS_AT_ONCE), ROWS_AT_ONCE))

    loaded, got_two, got_one = set(), set(), set()

    def wait_load(i):
        if i not in loaded:
            loaded.add(i)
            loads[i].wait()

    def wait_two(p):
        if p not in got_two:
            got_two.add(p)
            two_back(p).wait_recv()

    def wait_one(p):
        if p not in got_one:
            got_one.add(p)
            one_back(p).wait_recv()

    def multiply(u):
        j = u % CHUNKS
        if u < CHUNKS:
            wait_load(u)
        else:
            for p in range(j * PER_CHUNK, (j + 1) * PER_CHUNK):
                (wait_two if u < 2 * CHUNKS else wait_one)(p)
        part[u] = jnp.zeros((2, STRIP, BLOCK), jnp.float32)

        @pl.loop(0, GRID_ROWS // KTILE)
        def _(k):
            ks = pl.ds(pl.multiple_of(k * KTILE, KTILE), KTILE)
            got = lax.dot_general(
                blocks[u, ks, :], both[ks, :], (((0,), (0,)), ((), ())),
                preferred_element_type=jnp.float32)
            part[u, 0] += got[:, :BLOCK]
            part[u, 1] += got[:, BLOCK:]

        to_sibling(u).start()

    def chip_sum(u):
        to_sibling(u).wait_recv()

        @pl.when(edge)
        def _():
            def body(rows):
                snd[0, u, rows, :] = part[u, core, rows, :] + sib_in[u, rows, :]
            by_rows(body)
            edge_to_inner(u).start()

    def pair_sum(u):
        @pl.when(inner)
        def _():
            edge_to_inner(u).wait_recv()

            def body(rows):
                snd[0, u, rows, :] = part[u, core, rows, :] + sib_in[u, rows, :] + rcv[0, u, rows, :]
            by_rows(body)
            inner_to_inner(u).start()

    def whole_sum(u):
        @pl.when(inner)
        def _():
            inner_to_inner(u).wait_recv()

            def body(rows):
                total = snd[0, u, rows, :] + rcv[1, u, rows, :]
                snd[1, u, rows, :] = total
                fin[u, rows, :] = total
            by_rows(body)
            inner_to_edge(u).start()
            fin_to_sibling(u).start()
            fin_to_out(u).start()

    def edge_result(u):
        @pl.when(edge)
        def _():
            inner_to_edge(u).wait_recv()

            def body(rows):
                fin[u, rows, :] = rcv[0, u, rows, :]
            by_rows(body)
            fin_to_sibling(u).start()
            fin_to_out(u).start()

    stage_of = (multiply, chip_sum, pair_sum, whole_sum, edge_result)
    todo = plan()
    sent_two = 0
    for p in range(PIECES):
        while sent_two < min(PIECES, 2 * p + 6):
            wait_load(sent_two // PER_CHUNK)
            two_back(sent_two).start()
            sent_two += 1
        wait_two(p)
        if p >= AHEAD:
            one_back(p - AHEAD).wait_send()
        one_back(p).start()
        wait_load(CHUNKS)
        wait_load(CHUNKS + 1)
        while todo and todo[0][0] <= p:
            _, stage, unit = todo.pop(0)
            stage_of[stage](unit)
    for _, stage, unit in todo:
        stage_of[stage](unit)

    for p in range(PIECES - AHEAD, PIECES):
        one_back(p).wait_send()
    for p in range(PIECES):
        two_back(p).wait_send()
    for u in range(UNITS):
        to_sibling(u).wait_send()
        fin_to_out(u).wait()
        fin_to_sibling(u).wait()

    @pl.when(edge)
    def _():
        for u in range(UNITS):
            edge_to_inner(u).wait_send()

    @pl.when(inner)
    def _():
        for u in range(UNITS):
            inner_to_inner(u).wait_send()
            inner_to_edge(u).wait_send()


def per_device(n_cols, orbitals, applied):
    f32, bf16 = jnp.float32, jnp.bfloat16
    dma = pltpu.SemaphoreType.DMA
    out = pl.pallas_call(
        functools.partial(kernel, n_cols),
        out_shape=jax.ShapeDtypeStruct((2, 3, BLOCK, BLOCK), f32),
        in_specs=[pl.BlockSpec(memory_space=pl.ANY)] * 2,
        out_specs=pl.BlockSpec(memory_space=pl.ANY),
        scratch_shapes=[
            pltpu.VMEM((3 * CHUNKS, GRID_ROWS, STRIP), bf16),
            pltpu.VMEM((GRID_ROWS, 2 * BLOCK), bf16),
            pltpu.VMEM((UNITS, 2, STRIP, BLOCK), f32),
            pltpu.VMEM((UNITS, STRIP, BLOCK), f32),
            pltpu.VMEM((2, UNITS, STRIP, BLOCK), f32),
            pltpu.VMEM((2, UNITS, STRIP, BLOCK), f32),
            pltpu.VMEM((UNITS, STRIP, BLOCK), f32),
            dma((CHUNKS + 2,)),
            dma((PIECES,)), dma((PIECES,)), dma((PIECES,)), dma((PIECES,)),
            dma((UNITS,)), dma((UNITS,)),
            dma((2, UNITS)), dma((2, UNITS)),
            dma((UNITS,)), dma((UNITS,)), dma((UNITS,)),
        ],
        compiler_params=pltpu.CompilerParams(
            collective_id=0, has_side_effects=True, vmem_limit_bytes=58 * 2**20),
    )(orbitals, applied)
    return jnp.swapaxes(out[0], 1, 2), out[1]


def solution(mesh):
    placed = (P("rows", "cols"), P("rows", "cols"))
    return jax.shard_map(
        functools.partial(per_device, mesh.shape["cols"]),
        mesh=mesh,
        in_specs=placed,
        out_specs=(P(None, "cols", None), P(None, "cols", None)),
        check_vma=False,
    )
```

```python
import functools

import jax
import jax.numpy as jnp
from jax import lax
from jax.experimental import pallas as pl
from jax.experimental.pallas import tpu as pltpu
from jax.sharding import PartitionSpec as P

BLOCK = 512
GRID_ROWS = 4096
STRIP = 128
CHUNKS = BLOCK // STRIP
PIECE = 512
PER_CHUNK = GRID_ROWS // PIECE
PIECES = CHUNKS * PER_CHUNK
ROUND_OF = (0, 2, 1)
UNITS = 3 * CHUNKS
LAST = UNITS - 1
HALVES = 2
AHEAD = 4
DIRECT = 4
LEAD = 6
SLOW_HOP = AHEAD + 2
FAST_HOP = 2
TILE = 16
MESSAGE = STRIP + HALVES * TILE
POWER_STEPS = 6
LOW = 2.0 ** -1.875
SPAN = 2.0 ** 1.875 - LOW
MESH = pl.DeviceIdType.MESH


def encode(value, inverse):
    code = LOW + (SPAN * inverse) * jnp.abs(value)
    for _ in range(POWER_STEPS):
        code = code * code
    return jnp.where(value < 0, -code, code).astype(jnp.bfloat16)


def decode(code, scale):
    code = code.astype(jnp.float32)
    root = jnp.abs(code)
    for _ in range(POWER_STEPS):
        root = lax.rsqrt(root)
    value = (root - LOW) * (scale * (1 / SPAN))
    return jnp.where(code < 0, -value, value)


def halves_of(u):
    return HALVES if u == LAST else 1


def plan():
    todo = []

    def reduce(u, at):
        for stage, delay in enumerate((0, SLOW_HOP, SLOW_HOP + FAST_HOP, 2 * SLOW_HOP + FAST_HOP)):
            for h in range(halves_of(u)):
                todo.append((at + delay, 1 + stage, 1 + stage, (u, h)))

    for u in range(CHUNKS):
        for k in range(PER_CHUNK):
            todo.append((u, 0, 0, (u, k)))
        reduce(u, u + 1)
    for group, when in ((1, lambda p: p // 2 + 4), (2, lambda p: p + AHEAD + 1)):
        for p in range(PIECES):
            todo.append((when(p), 0, 0, (group * CHUNKS + p // PER_CHUNK, p % PER_CHUNK)))
        for j in range(CHUNKS):
            reduce(group * CHUNKS + j, when((j + 1) * PER_CHUNK - 1) + 1)
    return sorted(todo)


def kernel(n_cols, x_ref, hx_ref, out_ref, blocks, both, part, sib_in, snd, rcv, fin,
           load_sem, r1_send, r1_recv, r2_send, r2_recv, sib_send, sib_recv,
           z_send, z_recv, fin_send, fin_recv, out_sem):
    row = lax.axis_index("rows")
    col = lax.axis_index("cols")
    core = lax.rem(row, 2)
    z = row // 2
    upper = lax.rem(col, 2)
    edge = jnp.logical_or(z == 0, z == 3)
    inner = jnp.logical_or(z == 1, z == 2)
    sibling = (row + 1 - 2 * core, col)
    beside = (row + 2 - 4 * lax.rem(z, 2), col)
    across = ((3 - z) * 2 + core, col)
    half = (row, col + 1 - 2 * upper)

    def shifted(by):
        return (row, lax.rem(col + n_cols + by, n_cols))

    loads = [pltpu.make_async_copy(x_ref, both.at[:, pl.ds(0, BLOCK)], load_sem.at[0]),
             pltpu.make_async_copy(hx_ref, both.at[:, pl.ds(BLOCK, BLOCK)], load_sem.at[1])]
    for j in range(CHUNKS):
        loads.append(pltpu.make_async_copy(
            x_ref.at[:, pl.ds(j * STRIP, STRIP)], blocks.at[j], load_sem.at[2 + j]))

    barrier = pltpu.get_barrier_semaphore()
    for device in (sibling, beside, across, shifted(1), shifted(-1), shifted(2), shifted(-2)):
        pl.semaphore_signal(barrier, inc=1, device_id=device, device_id_type=MESH)
    pl.semaphore_wait(barrier, 7)

    def piece(slot, p):
        return blocks.at[slot + p // PER_CHUNK, pl.ds((p % PER_CHUNK) * PIECE, PIECE)]

    def own(p):
        return x_ref.at[pl.ds((p % PER_CHUNK) * PIECE, PIECE), pl.ds((p // PER_CHUNK) * STRIP, STRIP)]

    def remote(src, dst, send, recv, device):
        return pltpu.make_async_remote_copy(
            src_ref=src, dst_ref=dst, send_sem=send, recv_sem=recv,
            device_id=device, device_id_type=MESH)

    def two_back(p):
        return remote(own(p), piece(CHUNKS, p), r2_send.at[p], r2_recv.at[p], shifted(2))

    def one_back(p):
        if p < DIRECT:
            return remote(own(p), piece(2 * CHUNKS, p), r1_send.at[p], r1_recv.at[p], shifted(1))
        return remote(piece(upper * CHUNKS, p), piece(2 * CHUNKS, p), r1_send.at[p], r1_recv.at[p], half)

    def to_sibling(u):
        return remote(part.at[u, 1 - core], sib_in.at[u], sib_send.at[u], sib_recv.at[u], sibling)

    def message(buffer, s, u, h):
        size = STRIP // halves_of(u) + TILE
        return buffer.at[s, u, pl.ds(h * size, size)]

    def edge_to_inner(u, h):
        return remote(message(snd, 0, u, h), message(rcv, 0, u, h),
                      z_send.at[0, u, h], z_recv.at[0, u, h], beside)

    def inner_to_inner(u, h):
        return remote(message(snd, 0, u, h), message(rcv, 1, u, h),
                      z_send.at[0, u, h], z_recv.at[1, u, h], across)

    def inner_to_edge(u, h):
        return remote(message(snd, 1, u, h), message(rcv, 0, u, h),
                      z_send.at[1, u, h], z_recv.at[0, u, h], beside)

    def result(u, h):
        size = STRIP // halves_of(u)
        return (fin.at[u, pl.ds(h * size, size)],
                out_ref.at[core, ROUND_OF[u // CHUNKS], pl.ds((u % CHUNKS) * STRIP + h * size, size)])

    def fin_to_sibling(u, h):
        return remote(*result(u, h), fin_send.at[u, h], fin_recv.at[u, h], sibling)

    def fin_to_out(u, h):
        return pltpu.make_async_copy(*result(u, h), out_sem.at[u, h])

    def tile(start, i):
        return pl.ds(pl.multiple_of(start + i * TILE, TILE), TILE)

    def tiles_of(u):
        return STRIP // halves_of(u) // TILE

    def starts(u, h):
        return h * STRIP // halves_of(u), h * (STRIP // halves_of(u) + TILE)

    def write_code(s, u, h, value_of):
        at, to = starts(u, h)

        def scan(i, top):
            value = value_of(i)
            part[u, core, tile(at, i), :] = value
            return jnp.maximum(top, jnp.abs(value))
        top = lax.fori_loop(0, tiles_of(u), scan, jnp.full((TILE, BLOCK), 1e-30, jnp.float32))
        scale = (top * (1 + 2.0 ** -7)).astype(jnp.bfloat16)
        snd[s, u, tile(to, tiles_of(u)), :] = scale
        inverse = 1 / scale.astype(jnp.float32)

        @pl.loop(0, tiles_of(u))
        def _(i):
            snd[s, u, tile(to, i), :] = encode(part[u, core, tile(at, i), :], inverse)

    def reader(buffer, s, u, h):
        _, to = starts(u, h)
        scale = buffer[s, u, tile(to, tiles_of(u)), :].astype(jnp.float32)
        return lambda i: decode(buffer[s, u, tile(to, i), :], scale)

    def core_sum(u, h):
        at, _ = starts(u, h)
        return lambda i: part[u, core, tile(at, i), :] + sib_in[u, tile(at, i), :]

    waited = set()

    def once(kind, p, wait):
        if (kind, p) not in waited:
            waited.add((kind, p))
            wait()

    def wait_load(i):
        once("load", i, loads[i].wait)

    def wait_piece(group, p):
        once(group, p, (two_back(p) if group == 1 else one_back(p)).wait_recv)

    def multiply(u, k):
        wait_load(0)
        wait_load(1)
        if u < CHUNKS:
            wait_load(2 + u)
        else:
            wait_piece(u // CHUNKS, u % CHUNKS * PER_CHUNK + k)
        rows = pl.ds(k * PIECE, PIECE)
        got = lax.dot_general(
            blocks[u, rows, :], both[rows, :], (((0,), (0,)), ((), ())),
            preferred_element_type=jnp.float32)
        for kind in range(2):
            term = got[:, kind * BLOCK:(kind + 1) * BLOCK]
            part[u, kind] = term if k == 0 else part[u, kind] + term
        if k == PER_CHUNK - 1:
            to_sibling(u).start()

    def chip_sum(u, h):
        once("sibling", u, to_sibling(u).wait_recv)

        @pl.when(edge)
        def _():
            write_code(0, u, h, core_sum(u, h))
            edge_to_inner(u, h).start()

    def pair_sum(u, h):
        @pl.when(inner)
        def _():
            edge_to_inner(u, h).wait_recv()
            mine, theirs = core_sum(u, h), reader(rcv, 0, u, h)
            write_code(0, u, h, lambda i: mine(i) + theirs(i))
            inner_to_inner(u, h).start()

    def finish(u, h, buffer, s):
        at, _ = starts(u, h)
        read = reader(buffer, s, u, h)

        @pl.loop(0, tiles_of(u))
        def _(i):
            fin[u, tile(at, i), :] = read(i)
        fin_to_sibling(u, h).start()
        fin_to_out(u, h).start()

    def whole_sum(u, h):
        @pl.when(inner)
        def _():
            inner_to_inner(u, h).wait_recv()
            mine, theirs = reader(snd, 0, u, h), reader(rcv, 1, u, h)
            write_code(1, u, h, lambda i: mine(i) + theirs(i))
            inner_to_edge(u, h).start()
            finish(u, h, snd, 1)

    def edge_result(u, h):
        @pl.when(edge)
        def _():
            inner_to_edge(u, h).wait_recv()
            finish(u, h, rcv, 0)

    stage_of = (multiply, chip_sum, pair_sum, whole_sum, edge_result)
    todo = plan()
    sent_two = 0
    for p in range(PIECES):
        if p >= DIRECT:
            if p // PER_CHUNK < CHUNKS:
                wait_load(2 + p // PER_CHUNK)
            wait_piece(1, p)
        if p >= AHEAD:
            one_back(p - AHEAD).wait_send()
        one_back(p).start()
        while sent_two < min(PIECES, 2 * p + LEAD):
            two_back(sent_two).start()
            sent_two += 1
        if p == 0:
            for load in loads:
                load.start()
        while todo and todo[0][0] <= p:
            _, _, stage, args = todo.pop(0)
            stage_of[stage](*args)
    for _, _, stage, args in todo:
        stage_of[stage](*args)

    for p in range(PIECES - AHEAD, PIECES):
        one_back(p).wait_send()
    for p in range(PIECES):
        two_back(p).wait_send()
    for u in range(UNITS):
        to_sibling(u).wait_send()
        for h in range(halves_of(u)):
            fin_to_out(u, h).wait()
            fin_to_sibling(u, h).wait()

    @pl.when(edge)
    def _():
        for u in range(UNITS):
            for h in range(halves_of(u)):
                edge_to_inner(u, h).wait_send()

    @pl.when(inner)
    def _():
        for u in range(UNITS):
            for h in range(halves_of(u)):
                inner_to_inner(u, h).wait_send()
                inner_to_edge(u, h).wait_send()


def place(step):
    return step // 3, step % 3


def spread(in_ref, gram_ref, ham_ref):
    step = pl.program_id(0)

    @pl.when(step < 3)
    def _():
        gram_ref[0] = in_ref[0, 0].T

    @pl.when(step >= 3)
    def _():
        ham_ref[0] = in_ref[0, 0]


def per_device(n_cols, orbitals, applied):
    f32, bf16 = jnp.float32, jnp.bfloat16
    dma = pltpu.SemaphoreType.DMA
    sums = pl.pallas_call(
        functools.partial(kernel, n_cols),
        out_shape=jax.ShapeDtypeStruct((2, 3, BLOCK, BLOCK), f32),
        in_specs=[pl.BlockSpec(memory_space=pl.ANY)] * 2,
        out_specs=pl.BlockSpec(memory_space=pl.ANY),
        scratch_shapes=[
            pltpu.VMEM((3 * CHUNKS, GRID_ROWS, STRIP), bf16),
            pltpu.VMEM((GRID_ROWS, 2 * BLOCK), bf16),
            pltpu.VMEM((UNITS, 2, STRIP, BLOCK), f32),
            pltpu.VMEM((UNITS, STRIP, BLOCK), f32),
            pltpu.VMEM((2, UNITS, MESSAGE, BLOCK), bf16),
            pltpu.VMEM((2, UNITS, MESSAGE, BLOCK), bf16),
            pltpu.VMEM((UNITS, STRIP, BLOCK), f32),
            dma((2 + CHUNKS,)),
            dma((PIECES,)), dma((PIECES,)), dma((PIECES,)), dma((PIECES,)),
            dma((UNITS,)), dma((UNITS,)),
            dma((2, UNITS, HALVES)), dma((2, UNITS, HALVES)),
            dma((UNITS, HALVES)), dma((UNITS, HALVES)), dma((UNITS, HALVES)),
        ],
        compiler_params=pltpu.CompilerParams(
            collective_id=0, has_side_effects=True, vmem_limit_bytes=56 * 2**20),
    )(orbitals, applied)
    block = (1, BLOCK, BLOCK)
    gram, ham = pl.pallas_call(
        spread,
        grid=(6,),
        out_shape=[jax.ShapeDtypeStruct((3, BLOCK, BLOCK), f32)] * 2,
        in_specs=[pl.BlockSpec((1,) + block, lambda s: (s // 3, s % 3, 0, 0))],
        out_specs=[pl.BlockSpec(block, lambda s: (jnp.minimum(s, 2), 0, 0)),
                   pl.BlockSpec(block, lambda s: (jnp.maximum(s - 3, 0), 0, 0))],
    )(sums)
    return gram, ham


def solution(mesh):
    placed = (P("rows", "cols"), P("rows", "cols"))
    return jax.shard_map(
        functools.partial(per_device, mesh.shape["cols"]),
        mesh=mesh,
        in_specs=placed,
        out_specs=(P(None, "cols", None), P(None, "cols", None)),
        check_vma=False,
    )
```

```python
import functools

import jax
import jax.numpy as jnp
from jax import lax
from jax.experimental import pallas as pl
from jax.experimental.pallas import tpu as pltpu
from jax.sharding import PartitionSpec as P

BLOCK = 512
GRID_ROWS = 4096
STRIP = 128
CHUNKS = BLOCK // STRIP
PIECE = 512
PER_CHUNK = GRID_ROWS // PIECE
PIECES = CHUNKS * PER_CHUNK
ROUND_OF = (0, 2, 1)
UNITS = 3 * CHUNKS
LAST = UNITS - 1
HALVES = 2
AHEAD = 5
DIRECT = 4
LEAD = 6
SLOW_HOP = AHEAD + 2
FAST_HOP = 2
TILE = 16
MESSAGE = STRIP + HALVES * TILE
POWER_STEPS = 6
LOW = 2.0 ** -1.875
SPAN = 2.0 ** 1.875 - LOW
MESH = pl.DeviceIdType.MESH


def encode(value, inverse):
    code = LOW + (SPAN * inverse) * jnp.abs(value)
    for _ in range(POWER_STEPS):
        code = code * code
    return jnp.where(value < 0, -code, code).astype(jnp.bfloat16)


def decode(code, scale):
    code = code.astype(jnp.float32)
    root = jnp.abs(code)
    for _ in range(POWER_STEPS):
        root = lax.rsqrt(root)
    value = (root - LOW) * (scale * (1 / SPAN))
    return jnp.where(code < 0, -value, value)


def halves_of(u):
    return HALVES if u == LAST else 1


def plan():
    todo = []

    def reduce(u, at):
        for stage, delay in enumerate((0, SLOW_HOP, SLOW_HOP + FAST_HOP, 2 * SLOW_HOP + FAST_HOP)):
            for h in range(halves_of(u)):
                todo.append((at + delay, 1 + stage, 1 + stage, (u, h)))

    for u in range(CHUNKS):
        todo.append((u, 0, 0, (u, 0, PER_CHUNK)))
        reduce(u, u + 1)
    for group, when in ((1, lambda p: p // 2 + 4), (2, lambda p: p + AHEAD + 1)):
        for j in range(CHUNKS):
            u = group * CHUNKS + j
            cuts = (0, PER_CHUNK - 2, PER_CHUNK) if u == LAST else (0, PER_CHUNK)
            for start, stop in zip(cuts, cuts[1:]):
                todo.append((when(j * PER_CHUNK + stop - 1), 0, 0, (u, start, stop)))
            reduce(u, when((j + 1) * PER_CHUNK - 1) + 1)
    return sorted(todo)


def kernel(n_cols, x_ref, hx_ref, out_ref, blocks, both, part, sib_in, snd, rcv, fin,
           load_sem, r1_send, r1_recv, r2_send, r2_recv, sib_send, sib_recv,
           z_send, z_recv, fin_send, fin_recv, out_sem):
    row = lax.axis_index("rows")
    col = lax.axis_index("cols")
    core = lax.rem(row, 2)
    z = row // 2
    upper = lax.rem(col, 2)
    edge = jnp.logical_or(z == 0, z == 3)
    inner = jnp.logical_or(z == 1, z == 2)
    sibling = (row + 1 - 2 * core, col)
    beside = (row + 2 - 4 * lax.rem(z, 2), col)
    across = ((3 - z) * 2 + core, col)
    half = (row, col + 1 - 2 * upper)

    def shifted(by):
        return (row, lax.rem(col + n_cols + by, n_cols))

    loads = [pltpu.make_async_copy(x_ref, both.at[:, pl.ds(0, BLOCK)], load_sem.at[0]),
             pltpu.make_async_copy(hx_ref, both.at[:, pl.ds(BLOCK, BLOCK)], load_sem.at[1])]
    for j in range(CHUNKS):
        loads.append(pltpu.make_async_copy(
            x_ref.at[:, pl.ds(j * STRIP, STRIP)], blocks.at[j], load_sem.at[2 + j]))

    barrier = pltpu.get_barrier_semaphore()
    for device in (sibling, beside, across, shifted(1), shifted(-1), shifted(2), shifted(-2)):
        pl.semaphore_signal(barrier, inc=1, device_id=device, device_id_type=MESH)
    pl.semaphore_wait(barrier, 7)

    def piece(slot, p):
        return blocks.at[slot + p // PER_CHUNK, pl.ds((p % PER_CHUNK) * PIECE, PIECE)]

    def own(p):
        return x_ref.at[pl.ds((p % PER_CHUNK) * PIECE, PIECE), pl.ds((p // PER_CHUNK) * STRIP, STRIP)]

    def remote(src, dst, send, recv, device):
        return pltpu.make_async_remote_copy(
            src_ref=src, dst_ref=dst, send_sem=send, recv_sem=recv,
            device_id=device, device_id_type=MESH)

    def two_back(p):
        return remote(own(p), piece(CHUNKS, p), r2_send.at[p], r2_recv.at[p], shifted(2))

    def one_back(p):
        if p < DIRECT:
            return remote(own(p), piece(2 * CHUNKS, p), r1_send.at[p], r1_recv.at[p], shifted(1))
        return remote(piece(upper * CHUNKS, p), piece(2 * CHUNKS, p), r1_send.at[p], r1_recv.at[p], half)

    def to_sibling(u):
        return remote(part.at[u, 1 - core], sib_in.at[u], sib_send.at[u], sib_recv.at[u], sibling)

    def message(buffer, s, u, h):
        size = STRIP // halves_of(u) + TILE
        return buffer.at[s, u, pl.ds(h * size, size)]

    def edge_to_inner(u, h):
        return remote(message(snd, 0, u, h), message(rcv, 0, u, h),
                      z_send.at[0, u, h], z_recv.at[0, u, h], beside)

    def inner_to_inner(u, h):
        return remote(message(snd, 0, u, h), message(rcv, 1, u, h),
                      z_send.at[0, u, h], z_recv.at[1, u, h], across)

    def inner_to_edge(u, h):
        return remote(message(snd, 1, u, h), message(rcv, 0, u, h),
                      z_send.at[1, u, h], z_recv.at[0, u, h], beside)

    def result(u, h):
        size = STRIP // halves_of(u)
        return (fin.at[u, pl.ds(h * size, size)],
                out_ref.at[core, ROUND_OF[u // CHUNKS], pl.ds((u % CHUNKS) * STRIP + h * size, size)])

    def fin_to_sibling(u, h):
        return remote(*result(u, h), fin_send.at[u, h], fin_recv.at[u, h], sibling)

    def fin_to_out(u, h):
        return pltpu.make_async_copy(*result(u, h), out_sem.at[u, h])

    def tile(start, i):
        return pl.ds(pl.multiple_of(start + i * TILE, TILE), TILE)

    def tiles_of(u):
        return STRIP // halves_of(u) // TILE

    def starts(u, h):
        return h * STRIP // halves_of(u), h * (STRIP // halves_of(u) + TILE)

    def write_code(s, u, h, value_of):
        at, to = starts(u, h)

        def scan(i, top):
            value = value_of(i)
            part[u, core, tile(at, i), :] = value
            return jnp.maximum(top, jnp.abs(value))
        top = lax.fori_loop(0, tiles_of(u), scan, jnp.full((TILE, BLOCK), 1e-30, jnp.float32))
        scale = (top * (1 + 2.0 ** -7)).astype(jnp.bfloat16)
        snd[s, u, tile(to, tiles_of(u)), :] = scale
        inverse = 1 / scale.astype(jnp.float32)

        @pl.loop(0, tiles_of(u))
        def _(i):
            snd[s, u, tile(to, i), :] = encode(part[u, core, tile(at, i), :], inverse)

    def reader(buffer, s, u, h):
        _, to = starts(u, h)
        scale = buffer[s, u, tile(to, tiles_of(u)), :].astype(jnp.float32)
        return lambda i: decode(buffer[s, u, tile(to, i), :], scale)

    def core_sum(u, h):
        at, _ = starts(u, h)
        return lambda i: part[u, core, tile(at, i), :] + sib_in[u, tile(at, i), :]

    waited = set()

    def once(kind, p, wait):
        if (kind, p) not in waited:
            waited.add((kind, p))
            wait()

    def wait_load(i):
        once("load", i, loads[i].wait)

    def wait_piece(group, p):
        once(group, p, (two_back(p) if group == 1 else one_back(p)).wait_recv)

    def multiply(u, start, stop):
        wait_load(0)
        wait_load(1)
        if u < CHUNKS:
            wait_load(2 + u)
        else:
            for k in range(start, stop):
                wait_piece(u // CHUNKS, u % CHUNKS * PER_CHUNK + k)
        if start == 0:
            part[u] = jnp.zeros((2, STRIP, BLOCK), jnp.float32)

        @pl.loop(start, stop)
        def _(k):
            rows = pl.ds(pl.multiple_of(k * PIECE, PIECE), PIECE)
            got = lax.dot_general(
                blocks[u, rows, :], both[rows, :], (((0,), (0,)), ((), ())),
                preferred_element_type=jnp.float32)
            for kind in range(2):
                part[u, kind] += got[:, kind * BLOCK:(kind + 1) * BLOCK]
        if stop == PER_CHUNK:
            to_sibling(u).start()

    def chip_sum(u, h):
        once("sibling", u, to_sibling(u).wait_recv)

        @pl.when(edge)
        def _():
            write_code(0, u, h, core_sum(u, h))
            edge_to_inner(u, h).start()

    def pair_sum(u, h):
        @pl.when(inner)
        def _():
            edge_to_inner(u, h).wait_recv()
            mine, theirs = core_sum(u, h), reader(rcv, 0, u, h)
            write_code(0, u, h, lambda i: mine(i) + theirs(i))
            inner_to_inner(u, h).start()

    def finish(u, h, buffer, s):
        at, _ = starts(u, h)
        read = reader(buffer, s, u, h)

        @pl.loop(0, tiles_of(u))
        def _(i):
            fin[u, tile(at, i), :] = read(i)
        fin_to_sibling(u, h).start()
        fin_to_out(u, h).start()

    def whole_sum(u, h):
        @pl.when(inner)
        def _():
            inner_to_inner(u, h).wait_recv()
            mine, theirs = reader(snd, 0, u, h), reader(rcv, 1, u, h)
            write_code(1, u, h, lambda i: mine(i) + theirs(i))
            inner_to_edge(u, h).start()
            finish(u, h, snd, 1)

    def edge_result(u, h):
        @pl.when(edge)
        def _():
            inner_to_edge(u, h).wait_recv()
            finish(u, h, rcv, 0)

    stage_of = (multiply, chip_sum, pair_sum, whole_sum, edge_result)
    todo = plan()
    sent_two = 0
    for p in range(PIECES):
        if p >= DIRECT:
            if p // PER_CHUNK < CHUNKS:
                wait_load(2 + p // PER_CHUNK)
            wait_piece(1, p)
        if p >= AHEAD:
            one_back(p - AHEAD).wait_send()
        one_back(p).start()
        while sent_two < min(PIECES, 2 * p + LEAD):
            two_back(sent_two).start()
            sent_two += 1
        if p == 0:
            for load in loads:
                load.start()
        while todo and todo[0][0] <= p:
            _, _, stage, args = todo.pop(0)
            stage_of[stage](*args)
    for _, _, stage, args in todo:
        stage_of[stage](*args)

    for p in range(PIECES - AHEAD, PIECES):
        one_back(p).wait_send()
    for p in range(PIECES):
        two_back(p).wait_send()
    for u in range(UNITS):
        to_sibling(u).wait_send()
        for h in range(halves_of(u)):
            fin_to_out(u, h).wait()
            fin_to_sibling(u, h).wait()

    @pl.when(edge)
    def _():
        for u in range(UNITS):
            for h in range(halves_of(u)):
                edge_to_inner(u, h).wait_send()

    @pl.when(inner)
    def _():
        for u in range(UNITS):
            for h in range(halves_of(u)):
                inner_to_inner(u, h).wait_send()
                inner_to_edge(u, h).wait_send()


def spread(in_ref, gram_ref, ham_ref, before, after, in_sem, out_sem):
    hams, ins, outs = [], [], []
    for r in range(3):
        ins.append(pltpu.make_async_copy(in_ref.at[0, r], before.at[r], in_sem.at[r]))
        outs.append(pltpu.make_async_copy(after.at[r], gram_ref.at[r], out_sem.at[r]))
        hams.append(pltpu.make_async_copy(in_ref.at[1, r], ham_ref.at[r], out_sem.at[3 + r]))
    for copy in ins + hams:
        copy.start()
    for r in range(3):
        ins[r].wait()
        after[r] = before[r].T
        outs[r].start()
    for copy in hams + outs:
        copy.wait()


def per_device(n_cols, orbitals, applied):
    f32, bf16 = jnp.float32, jnp.bfloat16
    dma = pltpu.SemaphoreType.DMA
    sums = pl.pallas_call(
        functools.partial(kernel, n_cols),
        out_shape=jax.ShapeDtypeStruct((2, 3, BLOCK, BLOCK), f32),
        in_specs=[pl.BlockSpec(memory_space=pl.ANY)] * 2,
        out_specs=pl.BlockSpec(memory_space=pl.ANY),
        scratch_shapes=[
            pltpu.VMEM((3 * CHUNKS, GRID_ROWS, STRIP), bf16),
            pltpu.VMEM((GRID_ROWS, 2 * BLOCK), bf16),
            pltpu.VMEM((UNITS, 2, STRIP, BLOCK), f32),
            pltpu.VMEM((UNITS, STRIP, BLOCK), f32),
            pltpu.VMEM((2, UNITS, MESSAGE, BLOCK), bf16),
            pltpu.VMEM((2, UNITS, MESSAGE, BLOCK), bf16),
            pltpu.VMEM((UNITS, STRIP, BLOCK), f32),
            dma((2 + CHUNKS,)),
            dma((PIECES,)), dma((PIECES,)), dma((PIECES,)), dma((PIECES,)),
            dma((UNITS,)), dma((UNITS,)),
            dma((2, UNITS, HALVES)), dma((2, UNITS, HALVES)),
            dma((UNITS, HALVES)), dma((UNITS, HALVES)), dma((UNITS, HALVES)),
        ],
        compiler_params=pltpu.CompilerParams(
            collective_id=0, has_side_effects=True, vmem_limit_bytes=56 * 2**20),
    )(orbitals, applied)
    gram, ham = pl.pallas_call(
        spread,
        out_shape=[jax.ShapeDtypeStruct((3, BLOCK, BLOCK), f32)] * 2,
        in_specs=[pl.BlockSpec(memory_space=pl.ANY)],
        out_specs=[pl.BlockSpec(memory_space=pl.ANY)] * 2,
        scratch_shapes=[pltpu.VMEM((3, BLOCK, BLOCK), f32), pltpu.VMEM((3, BLOCK, BLOCK), f32),
                        dma((3,)), dma((6,))],
        compiler_params=pltpu.CompilerParams(vmem_limit_bytes=24 * 2**20),
    )(sums)
    return gram, ham


def solution(mesh):
    placed = (P("rows", "cols"), P("rows", "cols"))
    return jax.shard_map(
        functools.partial(per_device, mesh.shape["cols"]),
        mesh=mesh,
        in_specs=placed,
        out_specs=(P(None, "cols", None), P(None, "cols", None)),
        check_vma=False,
    )
```

```python
import functools

import jax
import jax.numpy as jnp
from jax import lax
from jax.experimental import pallas as pl
from jax.experimental.pallas import tpu as pltpu
from jax.sharding import PartitionSpec as P

BLOCK = 512
GRID_ROWS = 4096
STRIP = 128
CHUNKS = BLOCK // STRIP
PIECE = 512
PER_CHUNK = GRID_ROWS // PIECE
PIECES = CHUNKS * PER_CHUNK
ROUND_OF = (0, 2, 1)
UNITS = 3 * CHUNKS
LAST = UNITS - 1
HALVES = 2
AHEAD = 5
DIRECT = 4
LEAD = 6
SLOW_HOP = AHEAD + 1
FAST_HOP = 2
TILE = 16
MESSAGE = STRIP + HALVES * TILE
POWER_STEPS = 6
LOW = 2.0 ** -1.875
SPAN = 2.0 ** 1.875 - LOW
MESH = pl.DeviceIdType.MESH


def encode(value, inverse):
    code = LOW + (SPAN * inverse) * jnp.abs(value)
    for _ in range(POWER_STEPS):
        code = code * code
    return jnp.where(value < 0, -code, code).astype(jnp.bfloat16)


def decode(code, scale):
    code = code.astype(jnp.float32)
    root = jnp.abs(code)
    for _ in range(POWER_STEPS):
        root = lax.rsqrt(root)
    value = (root - LOW) * (scale * (1 / SPAN))
    return jnp.where(code < 0, -value, value)


def halves_of(u):
    return HALVES if u == LAST else 1


def plan():
    todo = []

    def reduce(u, at):
        for stage, delay in enumerate((0, SLOW_HOP, SLOW_HOP + FAST_HOP, 2 * SLOW_HOP + FAST_HOP)):
            for h in range(halves_of(u)):
                todo.append((at + delay, 1 + stage, 1 + stage, (u, h)))

    for u in range(CHUNKS):
        todo.append((u, 0, 0, (u, 0, PER_CHUNK)))
        reduce(u, u + 1)
    for group, when in ((1, lambda p: p // 2 + 4), (2, lambda p: p + AHEAD + 1)):
        for j in range(CHUNKS):
            u = group * CHUNKS + j
            cuts = (0, PER_CHUNK - 2, PER_CHUNK) if u == LAST else (0, PER_CHUNK)
            for start, stop in zip(cuts, cuts[1:]):
                todo.append((when(j * PER_CHUNK + stop - 1), 0, 0, (u, start, stop)))
            reduce(u, when((j + 1) * PER_CHUNK - 1) + 1)
    return sorted(todo)


def kernel(n_cols, x_ref, hx_ref, out_ref, blocks, both, part, sib_in, snd, rcv, fin,
           load_sem, r1_send, r1_recv, r2_send, r2_recv, sib_send, sib_recv,
           z_send, z_recv, fin_send, fin_recv, out_sem):
    row = lax.axis_index("rows")
    col = lax.axis_index("cols")
    core = lax.rem(row, 2)
    z = row // 2
    upper = lax.rem(col, 2)
    edge = jnp.logical_or(z == 0, z == 3)
    inner = jnp.logical_or(z == 1, z == 2)
    sibling = (row + 1 - 2 * core, col)
    beside = (row + 2 - 4 * lax.rem(z, 2), col)
    across = ((3 - z) * 2 + core, col)
    half = (row, col + 1 - 2 * upper)

    def shifted(by):
        return (row, lax.rem(col + n_cols + by, n_cols))

    loads = [pltpu.make_async_copy(x_ref, both.at[:, pl.ds(0, BLOCK)], load_sem.at[0]),
             pltpu.make_async_copy(hx_ref, both.at[:, pl.ds(BLOCK, BLOCK)], load_sem.at[1])]
    for j in range(CHUNKS):
        loads.append(pltpu.make_async_copy(
            x_ref.at[:, pl.ds(j * STRIP, STRIP)], blocks.at[j], load_sem.at[2 + j]))

    barrier = pltpu.get_barrier_semaphore()
    for device in (sibling, beside, across, shifted(1), shifted(-1), shifted(2), shifted(-2)):
        pl.semaphore_signal(barrier, inc=1, device_id=device, device_id_type=MESH)
    pl.semaphore_wait(barrier, 7)

    def piece(slot, p):
        return blocks.at[slot + p // PER_CHUNK, pl.ds((p % PER_CHUNK) * PIECE, PIECE)]

    def own(p):
        return x_ref.at[pl.ds((p % PER_CHUNK) * PIECE, PIECE), pl.ds((p // PER_CHUNK) * STRIP, STRIP)]

    def remote(src, dst, send, recv, device):
        return pltpu.make_async_remote_copy(
            src_ref=src, dst_ref=dst, send_sem=send, recv_sem=recv,
            device_id=device, device_id_type=MESH)

    def two_back(p):
        return remote(own(p), piece(CHUNKS, p), r2_send.at[p], r2_recv.at[p], shifted(2))

    def one_back(p):
        if p < DIRECT:
            return remote(own(p), piece(2 * CHUNKS, p), r1_send.at[p], r1_recv.at[p], shifted(1))
        return remote(piece(upper * CHUNKS, p), piece(2 * CHUNKS, p), r1_send.at[p], r1_recv.at[p], half)

    def to_sibling(u):
        return remote(part.at[u, 1 - core], sib_in.at[u], sib_send.at[u], sib_recv.at[u], sibling)

    def message(buffer, s, u, h):
        size = STRIP // halves_of(u) + TILE
        return buffer.at[s, u, pl.ds(h * size, size)]

    def edge_to_inner(u, h):
        return remote(message(snd, 0, u, h), message(rcv, 0, u, h),
                      z_send.at[0, u, h], z_recv.at[0, u, h], beside)

    def inner_to_inner(u, h):
        return remote(message(snd, 0, u, h), message(rcv, 1, u, h),
                      z_send.at[0, u, h], z_recv.at[1, u, h], across)

    def inner_to_edge(u, h):
        return remote(message(snd, 1, u, h), message(rcv, 0, u, h),
                      z_send.at[1, u, h], z_recv.at[0, u, h], beside)

    def result(u, h):
        size = STRIP // halves_of(u)
        return (fin.at[u, pl.ds(h * size, size)],
                out_ref.at[core, ROUND_OF[u // CHUNKS], pl.ds((u % CHUNKS) * STRIP + h * size, size)])

    def fin_to_sibling(u, h):
        return remote(*result(u, h), fin_send.at[u, h], fin_recv.at[u, h], sibling)

    def fin_to_out(u, h):
        return pltpu.make_async_copy(*result(u, h), out_sem.at[u, h])

    def tile(start, i):
        return pl.ds(pl.multiple_of(start + i * TILE, TILE), TILE)

    def tiles_of(u):
        return STRIP // halves_of(u) // TILE

    def starts(u, h):
        return h * STRIP // halves_of(u), h * (STRIP // halves_of(u) + TILE)

    def write_code(s, u, h, value_of):
        at, to = starts(u, h)

        def scan(i, top):
            value = value_of(i)
            part[u, core, tile(at, i), :] = value
            return jnp.maximum(top, jnp.abs(value))
        top = lax.fori_loop(0, tiles_of(u), scan, jnp.full((TILE, BLOCK), 1e-30, jnp.float32))
        scale = (top * (1 + 2.0 ** -7)).astype(jnp.bfloat16)
        snd[s, u, tile(to, tiles_of(u)), :] = scale
        inverse = 1 / scale.astype(jnp.float32)

        @pl.loop(0, tiles_of(u))
        def _(i):
            snd[s, u, tile(to, i), :] = encode(part[u, core, tile(at, i), :], inverse)

    def reader(buffer, s, u, h):
        _, to = starts(u, h)
        scale = buffer[s, u, tile(to, tiles_of(u)), :].astype(jnp.float32)
        return lambda i: decode(buffer[s, u, tile(to, i), :], scale)

    def core_sum(u, h):
        at, _ = starts(u, h)
        return lambda i: part[u, core, tile(at, i), :] + sib_in[u, tile(at, i), :]

    waited = set()

    def once(kind, p, wait):
        if (kind, p) not in waited:
            waited.add((kind, p))
            wait()

    def wait_load(i):
        once("load", i, loads[i].wait)

    def wait_piece(group, p):
        once(group, p, (two_back(p) if group == 1 else one_back(p)).wait_recv)

    def multiply(u, start, stop):
        wait_load(0)
        wait_load(1)
        if u < CHUNKS:
            wait_load(2 + u)
        else:
            for k in range(start, stop):
                wait_piece(u // CHUNKS, u % CHUNKS * PER_CHUNK + k)
        if start == 0:
            part[u] = jnp.zeros((2, STRIP, BLOCK), jnp.float32)

        @pl.loop(start, stop)
        def _(k):
            rows = pl.ds(pl.multiple_of(k * PIECE, PIECE), PIECE)
            got = lax.dot_general(
                blocks[u, rows, :], both[rows, :], (((0,), (0,)), ((), ())),
                preferred_element_type=jnp.float32)
            for kind in range(2):
                part[u, kind] += got[:, kind * BLOCK:(kind + 1) * BLOCK]
        if stop == PER_CHUNK:
            to_sibling(u).start()

    def chip_sum(u, h):
        once("sibling", u, to_sibling(u).wait_recv)

        @pl.when(edge)
        def _():
            write_code(0, u, h, core_sum(u, h))
            edge_to_inner(u, h).start()

    def pair_sum(u, h):
        @pl.when(inner)
        def _():
            edge_to_inner(u, h).wait_recv()
            mine, theirs = core_sum(u, h), reader(rcv, 0, u, h)
            write_code(0, u, h, lambda i: mine(i) + theirs(i))
            inner_to_inner(u, h).start()

    def finish(u, h, buffer, s):
        at, _ = starts(u, h)
        read = reader(buffer, s, u, h)

        @pl.loop(0, tiles_of(u))
        def _(i):
            fin[u, tile(at, i), :] = read(i)
        fin_to_sibling(u, h).start()
        fin_to_out(u, h).start()

    def whole_sum(u, h):
        @pl.when(inner)
        def _():
            inner_to_inner(u, h).wait_recv()
            mine, theirs = reader(snd, 0, u, h), reader(rcv, 1, u, h)
            write_code(1, u, h, lambda i: mine(i) + theirs(i))
            inner_to_edge(u, h).start()
            finish(u, h, snd, 1)

    def edge_result(u, h):
        @pl.when(edge)
        def _():
            inner_to_edge(u, h).wait_recv()
            finish(u, h, rcv, 0)

    stage_of = (multiply, chip_sum, pair_sum, whole_sum, edge_result)
    todo = plan()
    sent_two = 0
    for p in range(PIECES):
        if p >= DIRECT:
            if p // PER_CHUNK < CHUNKS:
                wait_load(2 + p // PER_CHUNK)
            wait_piece(1, p)
        if p >= AHEAD:
            one_back(p - AHEAD).wait_send()
        one_back(p).start()
        while sent_two < min(PIECES, 2 * p + LEAD):
            two_back(sent_two).start()
            sent_two += 1
        if p == 0:
            for load in loads:
                load.start()
        while todo and todo[0][0] <= p:
            _, _, stage, args = todo.pop(0)
            stage_of[stage](*args)
    for _, _, stage, args in todo:
        stage_of[stage](*args)

    for p in range(PIECES - AHEAD, PIECES):
        one_back(p).wait_send()
    for p in range(PIECES):
        two_back(p).wait_send()
    for u in range(UNITS):
        to_sibling(u).wait_send()
        for h in range(halves_of(u)):
            fin_to_out(u, h).wait()
            fin_to_sibling(u, h).wait()

    @pl.when(edge)
    def _():
        for u in range(UNITS):
            for h in range(halves_of(u)):
                edge_to_inner(u, h).wait_send()

    @pl.when(inner)
    def _():
        for u in range(UNITS):
            for h in range(halves_of(u)):
                inner_to_inner(u, h).wait_send()
                inner_to_edge(u, h).wait_send()


def spread(in_ref, gram_ref, ham_ref, before, after, in_sem, out_sem):
    hams, ins, outs = [], [], []
    for r in range(3):
        ins.append(pltpu.make_async_copy(in_ref.at[0, r], before.at[r], in_sem.at[r]))
        outs.append(pltpu.make_async_copy(after.at[r], gram_ref.at[r], out_sem.at[r]))
        hams.append(pltpu.make_async_copy(in_ref.at[1, r], ham_ref.at[r], out_sem.at[3 + r]))
    for copy in ins + hams:
        copy.start()
    for r in range(3):
        ins[r].wait()
        after[r] = before[r].T
        outs[r].start()
    for copy in hams + outs:
        copy.wait()


def per_device(n_cols, orbitals, applied):
    f32, bf16 = jnp.float32, jnp.bfloat16
    dma = pltpu.SemaphoreType.DMA
    sums = pl.pallas_call(
        functools.partial(kernel, n_cols),
        out_shape=jax.ShapeDtypeStruct((2, 3, BLOCK, BLOCK), f32),
        in_specs=[pl.BlockSpec(memory_space=pl.ANY)] * 2,
        out_specs=pl.BlockSpec(memory_space=pl.ANY),
        scratch_shapes=[
            pltpu.VMEM((3 * CHUNKS, GRID_ROWS, STRIP), bf16),
            pltpu.VMEM((GRID_ROWS, 2 * BLOCK), bf16),
            pltpu.VMEM((UNITS, 2, STRIP, BLOCK), f32),
            pltpu.VMEM((UNITS, STRIP, BLOCK), f32),
            pltpu.VMEM((2, UNITS, MESSAGE, BLOCK), bf16),
            pltpu.VMEM((2, UNITS, MESSAGE, BLOCK), bf16),
            pltpu.VMEM((UNITS, STRIP, BLOCK), f32),
            dma((2 + CHUNKS,)),
            dma((PIECES,)), dma((PIECES,)), dma((PIECES,)), dma((PIECES,)),
            dma((UNITS,)), dma((UNITS,)),
            dma((2, UNITS, HALVES)), dma((2, UNITS, HALVES)),
            dma((UNITS, HALVES)), dma((UNITS, HALVES)), dma((UNITS, HALVES)),
        ],
        compiler_params=pltpu.CompilerParams(
            collective_id=0, has_side_effects=True, vmem_limit_bytes=56 * 2**20),
    )(orbitals, applied)
    gram, ham = pl.pallas_call(
        spread,
        out_shape=[jax.ShapeDtypeStruct((3, BLOCK, BLOCK), f32)] * 2,
        in_specs=[pl.BlockSpec(memory_space=pl.ANY)],
        out_specs=[pl.BlockSpec(memory_space=pl.ANY)] * 2,
        scratch_shapes=[pltpu.VMEM((3, BLOCK, BLOCK), f32), pltpu.VMEM((3, BLOCK, BLOCK), f32),
                        dma((3,)), dma((6,))],
        compiler_params=pltpu.CompilerParams(vmem_limit_bytes=24 * 2**20),
    )(sums)
    return gram, ham


def solution(mesh):
    placed = (P("rows", "cols"), P("rows", "cols"))
    return jax.shard_map(
        functools.partial(per_device, mesh.shape["cols"]),
        mesh=mesh,
        in_specs=placed,
        out_specs=(P(None, "cols", None), P(None, "cols", None)),
        check_vma=False,
    )
```
